256 devices in a mesh: leaf: 256 (over z, y, x, core).
Axes of the slice: x: 4, y: 4, z: 8, core: 2. Of those that a mesh axis runs over, the one named last changes fastest.
Arguments:
- rhs: float32 [262144, 128], P('leaf'), may hold values from -6 to 6
- proj_bases: float32 [5, 262144, 256], P(None, 'leaf'), may hold values from -6 to 6
- corr_bases: float32 [5, 262144, 256], P(None, 'leaf'), may hold values from -0.375 to 0.375
- cores: float32 [5, 8192, 512], P(None, 'leaf'), may hold values from -0.25 to 0.25
Outputs:
- solution: float32 [262144, 128], P('leaf')
The draws below stay inside these ranges and needn't reach their ends.
All inputs are finite; a program needn't handle non-finite values.
Results may differ from the reference program's by a relative error of at most 0.00017.
Values sent between devices are 32-bit elements; how exact they have to be, the bound alone decides.
A program may use at most 64 MiB of HBM per device.

```python
import jax
import jax.numpy as jnp
from jax import lax

ROWS_DEV = 1024
RANK = 256
NRHS = 128
LEVELS = 5
ROWS = 262144
CROWS = 32
N_LEAF = 256


def block_levels(rng, dims, pieces, smallest, top_value):
    def one(position, parts):
        draws = jax.random.uniform(jax.random.fold_in(jax.random.fold_in(rng, 6), position), (parts,), jnp.float32, smallest / len(pieces), top_value / len(pieces))
        return jnp.repeat(jnp.exp(draws), dims[position] // parts).reshape((-1,) + (1,) * (len(dims) - position - 1))

    gain = one(*pieces[0])
    for cut in pieces[1:]:
        gain = gain * one(*cut)
    return gain


def gaussian(key, dims, scale, bound, pieces=(), held_as=jnp.bfloat16):
    values = jax.random.normal(key, dims, jnp.float32) * scale
    if len(pieces) > 0:
        values = block_levels(key, dims, pieces, -0.22, 0.18) * values
    return jnp.clip(values, min=-bound, max=bound).astype(held_as)


def setup_inputs(seed: int = 0) -> dict:
    key_list = jax.random.split(jax.random.key(seed), 5)
    rhs = gaussian(key_list[0], (ROWS, NRHS), 1.0, 6.0, ((0, 256),), jnp.float32)
    proj_bases = gaussian(key_list[1], (LEVELS, ROWS, RANK), 1.0, 6.0, ((1, 256),), jnp.float32)
    corr_bases = gaussian(key_list[2], (LEVELS, ROWS, RANK), RANK ** -0.5, 0.375, ((1, 256),), jnp.float32)
    cores = gaussian(key_list[3], (LEVELS, N_LEAF * CROWS, 2 * RANK), (2 * RANK) ** -0.5, 0.25, ((1, 256),), jnp.float32)
    return dict(rhs=rhs, proj_bases=proj_bases, corr_bases=corr_bases, cores=cores)


def reference(rhs, proj_bases, corr_bases, cores):
    highest = lax.Precision.HIGHEST
    x = rhs.reshape(N_LEAF, ROWS_DEV, NRHS)
    for j in reversed(range(LEVELS)):
        span = N_LEAF >> j
        half = span // 2
        nodes = N_LEAF // span
        used = RANK // half
        proj = proj_bases[j].reshape(N_LEAF, ROWS_DEV, RANK)
        corr = corr_bases[j].reshape(N_LEAF, ROWS_DEV, RANK)
        part = jnp.einsum('dnr,dnk->drk', proj, x, precision=highest)
        sums = part.reshape(nodes, 2, half, RANK, NRHS).sum(axis=2)
        z_all = sums.reshape(nodes, 2 * RANK, NRHS) / jnp.sqrt(jnp.float32(ROWS_DEV * half))
        table = cores[j].reshape(N_LEAF, CROWS, 2 * RANK)[:, :used, :]
        table = table.reshape(nodes, 2, RANK, 2 * RANK)
        t_all = jnp.einsum('ncab,nbk->ncak', table, z_all, precision=highest)
        t_dev = jnp.broadcast_to(t_all.reshape(nodes, 2, 1, RANK, NRHS), (nodes, 2, half, RANK, NRHS))
        t_dev = t_dev.reshape(N_LEAF, RANK, NRHS)
        x = x - jnp.einsum('dnr,drk->dnk', corr, t_dev, precision=highest)
    return x.reshape(ROWS_DEV * N_LEAF, NRHS)
```

```python
import functools

import jax
import jax.numpy as jnp
from jax import lax
from jax.experimental import pallas as pl
from jax.experimental.pallas import tpu as pltpu
from jax.sharding import PartitionSpec as P

f32, bf16 = jnp.float32, jnp.bfloat16
ROWS, RANK, COLS = 1024, 256, 128
MESH = pl.DeviceIdType.MESH

RING = list(range(1, 8))
XS = [2, 4, 6]
YS = [8, 16, 24]
YZ = [8, 16, 24, 32, 40, 48, 56]
ZS4 = [32, 64, 96]
ZS8 = [32 * k for k in range(1, 8)]
EXCHANGE = {4: [8], 3: YS, 2: YZ, 1: ZS4, 0: ZS8}
GREET = sorted(set(RING + YS + YZ + ZS8))
PIECES = {4: (1, 1, 4, 2, 32, 512), 3: (1, 2, 4, 2, 16, 512), 2: (1, 4, 4, 2, 8, 512),
          1: (2, 4, 4, 2, 8, 256), 0: (4, 4, 4, 2, 8, 128)}

NN = ((1,), (0,))
NT = ((1,), (1,))


def split(a):
    high = a.astype(bf16)
    return high, (a - high.astype(f32)).astype(bf16)


def mm(a, b, dims=NN):
    def one(u, v):
        return lax.dot_general(u, v, (dims, ((), ())), preferred_element_type=f32)
    return one(a[0], b[0]) + (one(a[0], b[1]) + one(a[1], b[0]))


class Sems:
    def __init__(self, send, recv):
        self.send, self.recv, self.used, self.copies = send, recv, 0, []


def kernel(nsem, rhs, proj, corr, cores, out, xin, pin, win, cst, xt, xts, x1, ps, wts, ws0,
           yb, rsb, sb, eb, tb, c4, c3, c2, c1, c0, chl, gloc, grh, gs1, gry, gs2, grx, gfin,
           g34, g23, y1e, outb, lsem, send_sem, recv_sem):
    me = lax.axis_index("leaf")
    h, x = me % 2, (me // 2) % 4
    y, z = (me // 8) % 4, me // 32
    s = me % 8
    cb = {4: c4, 3: c3, 2: c2, 1: c1, 0: c0}
    used = [0]
    everything = []

    def send(src, dst, mask):
        k = used[0]
        used[0] += 1
        copy = pltpu.make_async_remote_copy(
            src_ref=src, dst_ref=dst, send_sem=send_sem.at[k], recv_sem=recv_sem.at[k],
            device_id=(me ^ mask,), device_id_type=MESH)
        copy.start()
        everything.append(copy)
        return copy

    def landed(copies):
        for copy in copies:
            copy.wait_recv()

    nlocal = [0]

    def local(src, dst):
        copy = pltpu.make_async_copy(src, dst, lsem.at[nlocal[0]])
        nlocal[0] += 1
        copy.start()
        return copy

    own = {j: (z % PIECES[j][0], y % PIECES[j][1], x, h) for j in PIECES}
    lx = local(rhs, xin)
    lp, lw = {}, {}
    lp[4] = local(proj.at[4], pin.at[4])
    lc = {}
    for j in (4, 3, 2):
        lc[j] = local(cores.at[j, pl.ds(0, PIECES[j][4])], cb[j].at[own[j]])
    lc[1] = local(cores.at[1, pl.ds(0, 8)], cst.at[1])
    lc[0] = local(cores.at[0, pl.ds(0, 8)], cst.at[0])
    lp[3] = local(proj.at[3], pin.at[3])
    lw[4] = local(corr.at[4], win.at[4])
    for j, k in ((1, 2), (0, 1)):
        lp[j] = local(proj.at[j], pin.at[j])
        lw[k] = local(corr.at[k], win.at[k])
    lp[2] = local(proj.at[2], pin.at[2])
    lw[3] = local(corr.at[3], win.at[3])
    lw[0] = local(corr.at[0], win.at[0])

    barrier = pltpu.get_barrier_semaphore()
    for mask in GREET:
        pl.semaphore_signal(barrier, inc=1, device_id=(me ^ mask,), device_id_type=MESH)

    def ready_p(j):
        lp[j].wait()
        ps[j, 0], ps[j, 1] = split(pin[j])

    def ready_w(k):
        lw[k].wait()
        wts[k - 1, 0], wts[k - 1, 1] = split(win[k].T)

    def p(j):
        return ps[j, 0], ps[j, 1]

    def wt(k):
        return wts[k - 1, 0], wts[k - 1, 1]

    def state():
        return xts[0], xts[1]

    def set_state(value):
        xt[...] = value
        xts[0], xts[1] = split(value)

    def scatter(j):
        return [send(yb.at[j, pl.ds(pl.multiple_of((s ^ m) * 16, 16), 16)], rsb.at[j, m - 1], m)
                for m in RING]

    def ring_sum(j, copies):
        landed(copies)
        total = yb[j, pl.ds(pl.multiple_of(s * 16, 16), 16), :]
        for m in RING:
            total = total + rsb[j, m - 1]
        return total

    def exchange(j, value):
        sb[j] = value
        return [send(sb.at[j], eb.at[j, i], m) for i, m in enumerate(EXCHANGE[j])]

    def small(j, value, copies):
        landed(copies)
        count = len(EXCHANGE[j])
        mine = value
        for i in range(count // 2):
            mine = mine + eb[j, i]
        other = eb[j, count // 2]
        for i in range(count // 2 + 1, count):
            other = other + eb[j, i]
        bit = 7 - j
        left = (me >> bit) % 2 == 0
        scale = (ROWS << bit) ** -0.5
        zl = jnp.where(left, mine, other) * scale
        zr = jnp.where(left, other, mine) * scale
        return mm(split(jnp.concatenate([zl, zr], 1)), (chl[j, 0], chl[j, 1]), NT)

    def gather(j, t):
        rows = pl.ds(pl.multiple_of(s * 16, 16), 16)
        tb[j, rows, :] = t
        return [send(tb.at[j, rows], tb.at[j, rows], m) for m in RING]

    def core_x(j):
        lc[j].wait()
        if j == 1:
            cb[1][own[1]] = jnp.concatenate([cst[1, 0:4, 0:256], cst[1, 0:4, 256:512]], 0)
        if j == 0:
            cb[0][own[0]] = jnp.concatenate(
                [cst[0, 0:2, 128 * k:128 * k + 128] for k in range(4)], 0)
        return [send(cb[j].at[own[j]], cb[j].at[own[j]], m) for m in XS]

    def core_y(j, copies):
        landed(copies)
        view = cb[j].at[own[j][0], own[j][1], :, h]
        return [send(view, view, m) for m in YS[:PIECES[j][1] - 1]]

    def core_z(j, copies):
        landed(copies)
        view = cb[j].at[own[j][0], :, :, h]
        return [send(view, view, m) for m in ZS4[:PIECES[j][0] - 1]]

    def core_swap(j, copies):
        landed(copies)
        view = cb[j].at[:, :, :, h]
        return [send(view, view, 1)]

    def core_done(j, copies):
        landed(copies)
        value = cb[j][...]
        if j >= 2:
            chl[j, 0], chl[j, 1] = split(value.reshape(RANK, 2 * RANK))
            return
        width = PIECES[j][5]
        rows = 4 if j == 1 else 2
        value = value.reshape(RANK // 8, 8 // rows, 8, width)
        for k in range(512 // width):
            part = jnp.concatenate(
                [value[:, q, k * rows:(k + 1) * rows, :] for q in range(8 // rows)], 1)
            chl[j, 0, :, k * width:(k + 1) * width], chl[j, 1, :, k * width:(k + 1) * width] = (
                split(part.reshape(RANK, width)))

    lx.wait()
    set_state(xin[...].T)
    ready_p(4)
    yb[4] = mm(state(), p(4))
    pl.semaphore_wait(barrier, len(GREET))
    scatter4 = scatter(4)
    core4 = core_x(4)

    ready_p(3)
    yb[3] = mm(state(), p(3))
    ready_w(4)
    g34[...] = mm(wt(4), p(3))
    ready_p(1)
    ready_w(2)
    gloc[0] = mm(wt(2), p(1))

    sum4 = ring_sum(4, scatter4)
    exchange4 = exchange(4, sum4)
    core3 = core_x(3)
    core2 = core_x(2)
    core1 = core_x(1)
    core0 = core_x(0)
    ready_p(0)
    gloc[1] = mm(wt(2), p(0))
    core4 = core_swap(4, core4)
    ready_w(1)
    core_done(4, core4)
    t4 = small(4, sum4, exchange4)
    gather4 = gather(4, t4)

    gloc[2] = mm(wt(1), p(0))
    half_mine = pl.ds(pl.multiple_of(h * 128, 128), 128)
    half_other = pl.ds(pl.multiple_of((1 - h) * 128, 128), 128)
    graph = [send(gloc.at[:, half_other], grh, 1)]
    core3 = core_y(3, core3)
    core2 = core_y(2, core2)

    landed(gather4)
    g34s = split(g34[...])
    t4s = split(tb[4])
    yb[3] = yb[3] - mm(t4s, g34s)
    scatter3 = scatter(3)
    set_state(xt[...] - mm(t4s, wt(4)))
    ready_p(2)
    yb[2] = mm(state(), p(2))
    core3 = core_swap(3, core3)
    landed(graph)
    gs1[...] = gloc[:, half_mine, :] + grh[...]
    graph = [send(gs1.at[:, pl.ds(pl.multiple_of((y ^ (m // 8)) * 32, 32), 32)], gry.at[i], m)
             for i, m in enumerate(YS)]
    sum3 = ring_sum(3, scatter3)
    exchange3 = exchange(3, sum3)

    core1 = core_y(1, core1)
    core0 = core_y(0, core0)
    ready_w(3)
    g23[...] = mm(wt(3), p(2))
    core_done(3, core3)
    t3 = small(3, sum3, exchange3)
    gather3 = gather(3, t3)

    core2 = core_swap(2, core2)
    landed(graph)
    mine_y = pl.ds(pl.multiple_of(y * 32, 32), 32)
    gs2[...] = gs1[:, mine_y, :] + gry[0] + gry[1] + gry[2]
    graph = [send(gs2.at[:, pl.ds(pl.multiple_of((x ^ (m // 2)) * 8, 8), 8)], grx.at[i], m)
             for i, m in enumerate(XS)]
    core1 = core_z(1, core1)
    core0 = core_z(0, core0)
    g23s = split(g23[...])

    landed(gather3)
    t3s = split(tb[3])
    yb[2] = yb[2] - mm(t3s, g23s)
    scatter2 = scatter(2)
    set_state(xt[...] - mm(t3s, wt(3)))
    yb[1] = mm(state(), p(1))
    scatter1 = scatter(1)
    yb[0] = mm(state(), p(0))
    scatter0 = scatter(0)
    landed(graph)
    gfin[:, h, y, x] = (gs2[:, pl.ds(pl.multiple_of(x * 8, 8), 8), :]
                        + grx[0] + grx[1] + grx[2])
    graph = [send(gfin.at[:, h, y, x], gfin.at[:, h, y, x], m) for m in XS]
    core_done(2, core2)
    sum2 = ring_sum(2, scatter2)
    exchange2 = exchange(2, sum2)

    def plane_send(j, value):
        sb[j] = value
        return [send(sb.at[j], y1e.at[j, i], m) for i, m in enumerate(YS)]

    def plane_sum(j, value, copies):
        landed(copies)
        return value + y1e[j, 0] + y1e[j, 1] + y1e[j, 2]

    ring1 = ring_sum(1, scatter1)
    plane1 = plane_send(1, ring1)
    landed(graph)
    graph = [send(gfin.at[:, h, y], gfin.at[:, h, y], m) for m in YS]
    ring0 = ring_sum(0, scatter0)
    plane0 = plane_send(0, ring0)
    core1 = core_swap(1, core1)
    core0 = core_swap(0, core0)
    landed(graph)
    graph = [send(gfin.at[:, h], gfin.at[:, h], 1)]
    t2 = small(2, sum2, exchange2)
    t2s = split(t2)
    ring1 = plane_sum(1, ring1, plane1)
    landed(graph)

    def graph_of(g):
        return split(gfin[g].reshape(RANK, RANK))

    ring1 = ring1 - mm(t2s, graph_of(0))
    sb1 = outb
    sb1[0] = ring1
    exchange1 = [send(sb1.at[0], eb.at[1, i], m) for i, m in enumerate(EXCHANGE[1])]
    gather2 = gather(2, t2)
    core_done(1, core1)
    ring0 = plane_sum(0, ring0, plane0)
    ring0 = ring0 - mm(t2s, graph_of(1))
    core_done(0, core0)
    g01s = graph_of(2)
    t1 = small(1, ring1, exchange1)
    ring0 = ring0 - mm(split(t1), g01s)
    sb1[1] = ring0
    exchange0 = [send(sb1.at[1], eb.at[0, i], m) for i, m in enumerate(EXCHANGE[0])]
    gather1 = gather(1, t1)

    landed(gather2)
    set_state(xt[...] - mm(split(tb[2]), wt(2)))
    lw[0].wait()
    ws0[0], ws0[1] = split(win[0])
    landed(gather1)
    x1[...] = (xt[...] - mm(split(tb[1]), wt(1))).T
    t0 = small(0, ring0, exchange0)
    gather0 = gather(0, t0)
    landed(gather0)
    t0s = split(tb[0])
    parts = []
    for k in range(4):
        rows = pl.ds(256 * k, 256)
        x1[rows, :] = x1[rows, :] - mm((ws0[0, rows], ws0[1, rows]), t0s, NT)
        parts.append(local(x1.at[rows], out.at[rows]))
    for copy in everything:
        copy.wait_send()
    for copy in parts:
        copy.wait()
    assert used[0] == nsem, used[0]


NSEM = 145
NLOC = 20


def on_device(rhs, proj_bases, corr_bases, cores):
    any_space = pl.BlockSpec(memory_space=pl.ANY)
    v = pltpu.VMEM
    scratch = [
        v((ROWS, COLS), f32), v((5, ROWS, RANK), f32), v((5, ROWS, RANK), f32), v((2, 8, 512), f32),
        v((COLS, ROWS), f32), v((2, COLS, ROWS), bf16), v((ROWS, COLS), f32),
        v((5, 2, ROWS, RANK), bf16), v((4, 2, RANK, ROWS), bf16), v((2, ROWS, RANK), bf16),
        v((5, COLS, RANK), f32), v((5, 7, 16, RANK), f32), v((5, 16, RANK), f32),
        v((5, 7, 16, RANK), f32), v((5, COLS, RANK), f32),
        v(PIECES[4], f32), v(PIECES[3], f32), v(PIECES[2], f32), v(PIECES[1], f32), v(PIECES[0], f32),
        v((5, 2, RANK, 2 * RANK), bf16),
        v((3, RANK, RANK), f32), v((3, 128, RANK), f32), v((3, 128, RANK), f32),
        v((3, 3, 32, RANK), f32), v((3, 32, RANK), f32), v((3, 3, 8, RANK), f32),
        v((3, 2, 4, 4, 8, RANK), f32),
        v((RANK, RANK), f32), v((RANK, RANK), f32), v((2, 3, 16, RANK), f32), v((2, 16, RANK), f32),
        pltpu.SemaphoreType.DMA((NLOC,)), pltpu.SemaphoreType.DMA((NSEM,)), pltpu.SemaphoreType.DMA((NSEM,)),
    ]
    return pl.pallas_call(
        functools.partial(kernel, NSEM),
        out_shape=jax.ShapeDtypeStruct((ROWS, COLS), f32),
        in_specs=[any_space] * 4,
        out_specs=any_space,
        scratch_shapes=scratch,
        compiler_params=pltpu.CompilerParams(
            collective_id=0, has_side_effects=True, vmem_limit_bytes=56 << 20),
        cost_estimate=pl.CostEstimate(flops=1 << 31, bytes_accessed=12 << 20, transcendentals=0),
    )(rhs, proj_bases, corr_bases, cores)


def solution(mesh):
    return jax.shard_map(
        on_device,
        mesh=mesh,
        in_specs=(
            P("leaf", None),
            P(None, "leaf", None),
            P(None, "leaf", None),
            P(None, "leaf", None),
        ),
        out_specs=P("leaf", None),
        check_vma=False,
    )
```

```python
import functools

import jax
import jax.numpy as jnp
from jax import lax
from jax.experimental import pallas as pl
from jax.experimental.pallas import tpu as pltpu
from jax.sharding import PartitionSpec as P

f32, bf16 = jnp.float32, jnp.bfloat16
ROWS, RANK, COLS = 1024, 256, 128
MESH = pl.DeviceIdType.MESH

RING = list(range(1, 8))
XS = [2, 4, 6]
YS = [8, 16, 24]
YZ = [8, 16, 24, 32, 40, 48, 56]
ZS4 = [32, 64, 96]
ZS8 = [32 * k for k in range(1, 8)]
EXCHANGE = {4: [8], 3: YS, 2: YZ, 1: ZS4, 0: ZS8}
GREET = sorted(set(RING + YS + YZ + ZS8))
PIECES = {4: (1, 1, 4, 2, 32, 512), 3: (1, 2, 4, 2, 16, 512), 2: (1, 4, 4, 2, 8, 512),
          1: (2, 4, 4, 2, 8, 256), 0: (4, 4, 4, 2, 8, 128)}

NN = ((1,), (0,))
NT = ((1,), (1,))


def split(a):
    high = a.astype(bf16)
    return high, (a - high.astype(f32)).astype(bf16)


def mm(a, b, dims=NN):
    def one(u, v):
        return lax.dot_general(u, v, (dims, ((), ())), preferred_element_type=f32)
    return one(a[0], b[0]) + (one(a[0], b[1]) + one(a[1], b[0]))


def kernel(nsem, rhs, proj, corr, cores, out, xin, pin, win, cst, xt, xts, x1, ps, wts, ws0,
           yb, rsb, sb, eb, tb, c4, c3, c2, c1, c0, chl, g34, gloc, grh, gs1, gs2,
           rx23, rx13, rx03, gf23, gf13, gf03, py12, py0, px12, px0, pf12, pf0, y1e,
           lsem, send_sem, recv_sem):
    me = lax.axis_index("leaf")
    h, x = me % 2, (me // 2) % 4
    y, z = (me // 8) % 4, me // 32
    s = me % 8
    cb = {4: c4, 3: c3, 2: c2, 1: c1, 0: c0}
    used = [0]
    everything = []

    def send(src, dst, mask):
        k = used[0]
        used[0] += 1
        copy = pltpu.make_async_remote_copy(
            src_ref=src, dst_ref=dst, send_sem=send_sem.at[k], recv_sem=recv_sem.at[k],
            device_id=(me ^ mask,), device_id_type=MESH)
        copy.start()
        everything.append(copy)
        return copy

    def landed(copies):
        for copy in copies:
            copy.wait_recv()

    nlocal = [0]

    def local(src, dst):
        copy = pltpu.make_async_copy(src, dst, lsem.at[nlocal[0]])
        nlocal[0] += 1
        copy.start()
        return copy

    own = {j: (z % PIECES[j][0], y % PIECES[j][1], x, h) for j in PIECES}
    lp, lw, lc = {}, {}, {}

    def fetch_p(j):
        lp[j] = local(proj.at[j], pin.at[j])

    def fetch_w(k):
        lw[k] = local(corr.at[k], win.at[k])

    lx = local(rhs, xin)
    fetch_p(4)
    lc[4] = local(cores.at[4, pl.ds(0, 32)], c4.at[own[4]])
    fetch_p(1)
    fetch_w(2)
    fetch_p(0)
    fetch_w(1)
    fetch_p(2)
    fetch_w(3)
    lc[3] = local(cores.at[3, pl.ds(0, 16)], c3.at[own[3]])
    lc[2] = local(cores.at[2, pl.ds(0, 8)], c2.at[own[2]])
    lc[1] = local(cores.at[1, pl.ds(0, 8)], cst.at[1])
    lc[0] = local(cores.at[0, pl.ds(0, 8)], cst.at[0])
    fetch_p(3)
    fetch_w(4)
    fetch_w(0)

    barrier = pltpu.get_barrier_semaphore()
    for mask in GREET:
        pl.semaphore_signal(barrier, inc=1, device_id=(me ^ mask,), device_id_type=MESH)

    def ready_p(j):
        lp[j].wait()
        ps[j, 0], ps[j, 1] = split(pin[j])

    def ready_w(k):
        lw[k].wait()
        wts[k - 1, 0], wts[k - 1, 1] = split(win[k].T)

    def p(j):
        return ps[j, 0], ps[j, 1]

    def wt(k):
        return wts[k - 1, 0], wts[k - 1, 1]

    def state():
        return xts[0], xts[1]

    def set_state(value):
        xt[...] = value
        xts[0], xts[1] = split(value)

    def scatter(j):
        return [send(yb.at[j, pl.ds(pl.multiple_of((s ^ m) * 16, 16), 16)], rsb.at[j, m - 1], m)
                for m in RING]

    def ring_sum(j, copies):
        landed(copies)
        total = yb[j, pl.ds(pl.multiple_of(s * 16, 16), 16), :]
        for m in RING:
            total = total + rsb[j, m - 1]
        return total

    def exchange(j, value):
        sb[2 + j] = value
        return [send(sb.at[2 + j], eb.at[j, i], m) for i, m in enumerate(EXCHANGE[j])]

    def small(j, value, copies):
        landed(copies)
        count = len(EXCHANGE[j])
        mine = value
        for i in range(count // 2):
            mine = mine + eb[j, i]
        other = eb[j, count // 2]
        for i in range(count // 2 + 1, count):
            other = other + eb[j, i]
        bit = 7 - j
        left = (me >> bit) % 2 == 0
        scale = (ROWS << bit) ** -0.5
        zl = jnp.where(left, mine, other) * scale
        zr = jnp.where(left, other, mine) * scale
        return mm(split(jnp.concatenate([zl, zr], 1)), (chl[j, 0], chl[j, 1]), NT)

    def gather(j, t):
        rows = pl.ds(pl.multiple_of(s * 16, 16), 16)
        tb[j, rows, :] = t
        return [send(tb.at[j, rows], tb.at[j, rows], m) for m in RING]

    def core_x(j):
        lc[j].wait()
        if j == 1:
            cb[1][own[1]] = jnp.concatenate([cst[1, 0:4, 0:256], cst[1, 0:4, 256:512]], 0)
        if j == 0:
            cb[0][own[0]] = jnp.concatenate(
                [cst[0, 0:2, 128 * k:128 * k + 128] for k in range(4)], 0)
        return [send(cb[j].at[own[j]], cb[j].at[own[j]], m) for m in XS]

    def core_y(j, copies):
        landed(copies)
        view = cb[j].at[own[j][0], own[j][1], :, h]
        return [send(view, view, m) for m in YS[:PIECES[j][1] - 1]]

    def core_z(j, copies):
        landed(copies)
        view = cb[j].at[own[j][0], :, :, h]
        return [send(view, view, m) for m in ZS4[:PIECES[j][0] - 1]]

    def core_swap(j, copies):
        landed(copies)
        view = cb[j].at[:, :, :, h]
        return [send(view, view, 1)]

    def core_done(j, copies):
        landed(copies)
        value = cb[j][...]
        if j >= 2:
            chl[j, 0], chl[j, 1] = split(value.reshape(RANK, 2 * RANK))
            return
        width = PIECES[j][5]
        rows = 4 if j == 1 else 2
        value = value.reshape(RANK // 8, 8 // rows, 8, width)
        for k in range(512 // width):
            part = jnp.concatenate(
                [value[:, q, k * rows:(k + 1) * rows, :] for q in range(8 // rows)], 1)
            chl[j, 0, :, k * width:(k + 1) * width], chl[j, 1, :, k * width:(k + 1) * width] = (
                split(part.reshape(RANK, width)))

    half_mine = pl.ds(pl.multiple_of(h * 128, 128), 128)
    half_other = pl.ds(pl.multiple_of((1 - h) * 128, 128), 128)

    def graph_swap(span):
        return [send(gloc.at[span, half_other], grh.at[span], 1)]

    def chip_sum(span, copies):
        landed(copies)
        gs1[span] = gloc[span, half_mine, :] + grh[span]

    def piece(m, unit, size):
        at = x if unit == 2 else y
        return pl.ds(pl.multiple_of((at ^ (m // unit)) * size, size), size)

    def ring_scatter(span, copies, got):
        chip_sum(span, copies)
        return [send(gs1.at[span, piece(m, 2, 32)], got.at[i], m) for i, m in enumerate(XS)]

    def ring_gather(span, copies, got, full):
        landed(copies)
        full[:, h, x] = gs1[span, piece(0, 2, 32), :] + got[0] + got[1] + got[2]
        view = full.at[:, h, x]
        return [send(view, view, m) for m in XS]

    def plane_scatter_y(span, copies, got):
        chip_sum(span, copies)
        return [send(gs1.at[span, piece(m, 8, 32)], got.at[i], m) for i, m in enumerate(YS)]

    def plane_scatter_x(span, copies, got, got_x):
        landed(copies)
        gs2[span] = gs1[span, piece(0, 8, 32), :] + got[0] + got[1] + got[2]
        return [send(gs2.at[span, piece(m, 2, 8)], got_x.at[i], m) for i, m in enumerate(XS)]

    def plane_gather_x(span, copies, got_x, full):
        landed(copies)
        full[:, h, y, x] = gs2[span, piece(0, 2, 8), :] + got_x[0] + got_x[1] + got_x[2]
        view = full.at[:, h, y, x]
        return [send(view, view, m) for m in XS]

    def plane_gather_y(copies, full):
        landed(copies)
        view = full.at[:, h, y]
        return [send(view, view, m) for m in YS]

    def full_swap(copies, full):
        landed(copies)
        view = full.at[:, h]
        return [send(view, view, 1)]

    def whole(full, g):
        return split(full[g].reshape(RANK, RANK))

    def plane_send(j, value):
        sb[j] = value
        return [send(sb.at[j], y1e.at[j, i], m) for i, m in enumerate(YS)]

    def plane_sum(j, value, copies):
        landed(copies)
        return value + y1e[j, 0] + y1e[j, 1] + y1e[j, 2]

    def exchange_up(j, value):
        sb[2 + j] = value
        return [send(sb.at[2 + j], eb.at[j, i], m) for i, m in enumerate(EXCHANGE[j])]

    S12, S0, S23, S13, S03 = (pl.ds(0, 1), pl.ds(1, 2), pl.ds(3, 1), pl.ds(4, 1), pl.ds(5, 1))

    lx.wait()
    set_state(xin[...].T)
    ready_p(4)
    yb[4] = mm(state(), p(4))
    pl.semaphore_wait(barrier, len(GREET))
    scatter4 = scatter(4)
    core4 = core_x(4)

    ready_p(1)
    ready_w(2)
    gloc[0] = mm(wt(2), p(1))
    plane12 = graph_swap(S12)
    ready_p(0)
    gloc[1] = mm(wt(2), p(0))
    ready_w(1)
    gloc[2] = mm(wt(1), p(0))
    sum4 = ring_sum(4, scatter4)
    exchange4 = exchange(4, sum4)
    core3 = core_x(3)
    core2 = core_x(2)
    core1 = core_x(1)
    core0 = core_x(0)
    plane0s = graph_swap(S0)
    plane12 = plane_scatter_y(S12, plane12, py12)
    ready_p(2)
    ready_w(3)
    gloc[3] = mm(wt(3), p(2))
    ring23 = graph_swap(S23)
    core4 = core_swap(4, core4)
    gloc[4] = mm(wt(3), p(1))
    ring13 = graph_swap(S13)
    core_done(4, core4)
    t4 = small(4, sum4, exchange4)
    gather4 = gather(4, t4)

    ready_p(3)
    ring23 = ring_scatter(S23, ring23, rx23)
    yb[3] = mm(state(), p(3))
    ring13 = ring_scatter(S13, ring13, rx13)
    ready_w(4)
    g34[...] = mm(wt(4), p(3))
    plane12 = plane_scatter_x(S12, plane12, py12, px12)
    core3 = core_y(3, core3)
    plane0s = plane_scatter_y(S0, plane0s, py0)
    core2 = core_y(2, core2)

    g34s = split(g34[...])
    landed(gather4)
    t4s = split(tb[4])
    yb[3] = yb[3] - mm(t4s, g34s)
    scatter3 = scatter(3)
    set_state(xt[...] - mm(t4s, wt(4)))
    yb[2] = mm(state(), p(2))
    scatter2 = scatter(2)
    ring23 = ring_gather(S23, ring23, rx23, gf23)
    yb[1] = mm(state(), p(1))
    scatter1 = scatter(1)
    plane12 = plane_gather_x(S12, plane12, px12, pf12)
    yb[0] = mm(state(), p(0))
    scatter0 = scatter(0)
    ring13 = ring_gather(S13, ring13, rx13, gf13)
    sum3 = ring_sum(3, scatter3)
    exchange3 = exchange(3, sum3)

    core3 = core_swap(3, core3)
    gloc[5] = mm(wt(3), p(0))
    ring03 = graph_swap(S03)
    ring23 = full_swap(ring23, gf23)
    core1 = core_y(1, core1)
    core_done(3, core3)
    plane12 = plane_gather_y(plane12, pf12)
    ring03 = ring_scatter(S03, ring03, rx03)
    sum2 = ring_sum(2, scatter2)
    landed(ring23)
    g23s = whole(gf23, 0)
    t3 = small(3, sum3, exchange3)
    t3s = split(t3)

    sum2 = sum2 - mm(t3s, g23s)
    exchange2 = exchange(2, sum2)
    gather3 = gather(3, t3)
    core2 = core_swap(2, core2)
    plane0s = plane_scatter_x(S0, plane0s, py0, px0)
    core0 = core_y(0, core0)
    core1 = core_z(1, core1)
    ring13 = full_swap(ring13, gf13)
    ring1 = ring_sum(1, scatter1)
    landed(ring13)
    ring1 = ring1 - mm(t3s, whole(gf13, 0))
    plane1 = plane_send(1, ring1)
    ring03 = ring_gather(S03, ring03, rx03, gf03)
    plane12 = full_swap(plane12, pf12)
    core_done(2, core2)
    plane0s = plane_gather_x(S0, plane0s, px0, pf0)
    core0 = core_z(0, core0)
    landed(plane12)
    g12s = whole(pf12, 0)
    t2 = small(2, sum2, exchange2)
    t2s = split(t2)
    plane1 = plane_sum(1, ring1, plane1)
    plane1 = plane1 - mm(t2s, g12s)
    exchange1 = exchange_up(1, plane1)

    gather2 = gather(2, t2)
    ring03 = full_swap(ring03, gf03)
    plane0s = plane_gather_y(plane0s, pf0)
    core1 = core_swap(1, core1)
    ring0 = ring_sum(0, scatter0)
    landed(ring03)
    ring0 = ring0 - mm(t3s, whole(gf03, 0))
    plane0 = plane_send(0, ring0)
    core_done(1, core1)
    core0 = core_swap(0, core0)
    landed(gather3)
    set_state(xt[...] - mm(split(tb[3]), wt(3)))
    plane0s = full_swap(plane0s, pf0)
    t1 = small(1, plane1, exchange1)
    plane0 = plane_sum(0, ring0, plane0)
    landed(plane0s)
    plane0 = plane0 - mm(t2s, whole(pf0, 0)) - mm(split(t1), whole(pf0, 1))
    exchange0 = exchange_up(0, plane0)

    gather1 = gather(1, t1)
    landed(gather2)
    set_state(xt[...] - mm(split(tb[2]), wt(2)))
    lw[0].wait()
    ws0[0], ws0[1] = split(win[0])
    core_done(0, core0)
    landed(gather1)
    x1[...] = (xt[...] - mm(split(tb[1]), wt(1))).T
    t0 = small(0, plane0, exchange0)
    gather0 = gather(0, t0)
    for copy in everything[:-7]:
        copy.wait_send()
    landed(gather0)
    t0s = split(tb[0])
    parts = []
    for k in range(4):
        rows = pl.ds(256 * k, 256)
        x1[rows, :] = x1[rows, :] - mm((ws0[0, rows], ws0[1, rows]), t0s, NT)
        parts.append(local(x1.at[rows], out.at[rows]))
    for copy in everything[-7:]:
        copy.wait_send()
    for copy in parts:
        copy.wait()
    assert used[0] == nsem, used[0]


NSEM = 183
NLOC = 20


def on_device(rhs, proj_bases, corr_bases, cores):
    any_space = pl.BlockSpec(memory_space=pl.ANY)
    v = pltpu.VMEM
    scratch = [
        v((ROWS, COLS), f32), v((5, ROWS, RANK), f32), v((5, ROWS, RANK), f32), v((2, 8, 512), f32),
        v((COLS, ROWS), f32), v((2, COLS, ROWS), bf16), v((ROWS, COLS), f32),
        v((5, 2, ROWS, RANK), bf16), v((4, 2, RANK, ROWS), bf16), v((2, ROWS, RANK), bf16),
        v((5, COLS, RANK), f32), v((5, 7, 16, RANK), f32), v((7, 16, RANK), f32),
        v((5, 7, 16, RANK), f32), v((5, COLS, RANK), f32),
        v(PIECES[4], f32), v(PIECES[3], f32), v(PIECES[2], f32), v(PIECES[1], f32), v(PIECES[0], f32),
        v((5, 2, RANK, 2 * RANK), bf16),
        v((RANK, RANK), f32), v((6, RANK, RANK), f32), v((6, 128, RANK), f32),
        v((6, 128, RANK), f32), v((3, 32, RANK), f32),
        v((3, 1, 32, RANK), f32), v((3, 1, 32, RANK), f32), v((3, 1, 32, RANK), f32),
        v((1, 2, 4, 32, RANK), f32), v((1, 2, 4, 32, RANK), f32), v((1, 2, 4, 32, RANK), f32),
        v((3, 1, 32, RANK), f32), v((3, 2, 32, RANK), f32),
        v((3, 1, 8, RANK), f32), v((3, 2, 8, RANK), f32),
        v((1, 2, 4, 4, 8, RANK), f32), v((2, 2, 4, 4, 8, RANK), f32),
        v((2, 3, 16, RANK), f32),
        pltpu.SemaphoreType.DMA((NLOC,)), pltpu.SemaphoreType.DMA((NSEM,)), pltpu.SemaphoreType.DMA((NSEM,)),
    ]
    return pl.pallas_call(
        functools.partial(kernel, NSEM),
        out_shape=jax.ShapeDtypeStruct((ROWS, COLS), f32),
        in_specs=[any_space] * 4,
        out_specs=any_space,
        scratch_shapes=scratch,
        compiler_params=pltpu.CompilerParams(
            collective_id=0, has_side_effects=True, vmem_limit_bytes=56 << 20),
        cost_estimate=pl.CostEstimate(flops=1 << 31, bytes_accessed=12 << 20, transcendentals=0),
    )(rhs, proj_bases, corr_bases, cores)


def solution(mesh):
    return jax.shard_map(
        on_device,
        mesh=mesh,
        in_specs=(
            P("leaf", None),
            P(None, "leaf", None),
            P(None, "leaf", None),
            P(None, "leaf", None),
        ),
        out_specs=P("leaf", None),
        check_vma=False,
    )
```

```python
import functools

import jax
import jax.numpy as jnp
from jax import lax
from jax.experimental import pallas as pl
from jax.experimental.pallas import tpu as pltpu
from jax.sharding import PartitionSpec as P

f32, bf16 = jnp.float32, jnp.bfloat16
ROWS, RANK, COLS = 1024, 256, 128
MESH = pl.DeviceIdType.MESH

RING = list(range(1, 8))
XS = [2, 4, 6]
YS = [8, 16, 24]
YZ = [8, 16, 24, 32, 40, 48, 56]
ZS4 = [32, 64, 96]
ZS8 = [32 * k for k in range(1, 8)]
EXCHANGE = {4: [8], 3: YS, 2: YZ, 1: ZS4, 0: ZS8}
GREET = sorted(set(RING + YS + YZ + ZS8))
PIECES = {4: (1, 1, 4, 2, 32, 512), 3: (1, 2, 4, 2, 16, 512), 2: (1, 4, 4, 2, 8, 512),
          1: (2, 4, 4, 2, 8, 256), 0: (4, 4, 4, 2, 8, 128)}

NN = ((1,), (0,))
NT = ((1,), (1,))


def split(a):
    high = a.astype(bf16)
    return high, (a - high.astype(f32)).astype(bf16)


def mm(a, b, dims=NN):
    def one(u, v):
        return lax.dot_general(u, v, (dims, ((), ())), preferred_element_type=f32)
    return one(a[0], b[0]) + (one(a[0], b[1]) + one(a[1], b[0]))


def kernel(nsem, rhs, proj, corr, cores, out, xin, pin, win, cst, xt, xts, x1, ps, wts, ws0,
           yb, rsb, sb, eb, tb, c4, c3, c2, c1, c0, cht, g34, gloc, grh, gs1, gs2,
           rx23, rx13, rx03, gf23, gf13, gf03, py12, py0, px12, px0, pf12, pf0, y1e,
           lsem, send_sem, recv_sem):
    me = lax.axis_index("leaf")
    h, x = me % 2, (me // 2) % 4
    y, z = (me // 8) % 4, me // 32
    s = me % 8
    cb = {4: c4, 3: c3, 2: c2, 1: c1, 0: c0}
    used = [0]
    everything = []

    def send(parts, total):
        k = used[0]
        used[0] += 1

        def describe(src, dst, mask):
            return pltpu.make_async_remote_copy(
                src_ref=src, dst_ref=dst, send_sem=send_sem.at[k], recv_sem=recv_sem.at[k],
                device_id=(me ^ mask,), device_id_type=MESH)

        for part in parts:
            describe(*part).start()
        group = describe(total, total, parts[0][2])
        everything.append(group)
        return group

    def landed(group):
        if group is not None:
            group.wait_recv()

    nlocal = [0]

    def local(src, dst):
        copy = pltpu.make_async_copy(src, dst, lsem.at[nlocal[0]])
        nlocal[0] += 1
        copy.start()
        return copy

    own = {j: (z % PIECES[j][0], y % PIECES[j][1], x, h) for j in PIECES}
    lp, lw, lc = {}, {}, {}

    def fetch_p(j):
        lp[j] = local(proj.at[j], pin.at[j])

    def fetch_w(k):
        lw[k] = local(corr.at[k], win.at[k])

    lx = local(rhs, xin)
    fetch_p(4)
    lc[4] = local(cores.at[4, pl.ds(0, 32)], c4.at[own[4]])
    fetch_p(1)
    fetch_w(2)
    fetch_p(0)
    fetch_w(1)
    fetch_p(2)
    fetch_w(3)
    lc[3] = local(cores.at[3, pl.ds(0, 16)], c3.at[own[3]])
    lc[2] = local(cores.at[2, pl.ds(0, 8)], c2.at[own[2]])
    lc[1] = local(cores.at[1, pl.ds(0, 8)], cst.at[1])
    lc[0] = local(cores.at[0, pl.ds(0, 8)], cst.at[0])
    fetch_p(3)
    fetch_w(4)
    fetch_w(0)

    barrier = pltpu.get_barrier_semaphore()
    for mask in GREET:
        pl.semaphore_signal(barrier, inc=1, device_id=(me ^ mask,), device_id_type=MESH)

    def ready_p(j):
        lp[j].wait()
        ps[j, 0], ps[j, 1] = split(pin[j])

    def ready_w(k):
        lw[k].wait()
        wts[k - 1, 0], wts[k - 1, 1] = split(win[k].T)

    def p(j):
        return ps[j, 0], ps[j, 1]

    def wt(k):
        return wts[k - 1, 0], wts[k - 1, 1]

    def state():
        return xts[0], xts[1]

    def set_state(value):
        xt[...] = value
        xts[0], xts[1] = split(value)

    def scatter(j):
        return send([(yb.at[j, pl.ds(pl.multiple_of((s ^ m) * 16, 16), 16)], rsb.at[j, m - 1], m)
                     for m in RING], rsb.at[j])

    def ring_sum(j, copies):
        landed(copies)
        total = yb[j, pl.ds(pl.multiple_of(s * 16, 16), 16), :]
        for m in RING:
            total = total + rsb[j, m - 1]
        return total

    def exchange(j, value):
        sb[2 + j] = value
        return send([(sb.at[2 + j], eb.at[j, i], m) for i, m in enumerate(EXCHANGE[j])],
                    eb.at[j, pl.ds(0, len(EXCHANGE[j]))])

    def small(j, value, copies):
        landed(copies)
        count = len(EXCHANGE[j])
        mine = value
        for i in range(count // 2):
            mine = mine + eb[j, i]
        other = eb[j, count // 2]
        for i in range(count // 2 + 1, count):
            other = other + eb[j, i]
        bit = 7 - j
        left = (me >> bit) % 2 == 0
        scale = (ROWS << bit) ** -0.5
        zl = jnp.where(left, mine, other) * scale
        zr = jnp.where(left, other, mine) * scale
        return mm(split(jnp.concatenate([zl, zr], 1)), (cht[j, 0], cht[j, 1]))

    def gather(j, t):
        rows = pl.ds(pl.multiple_of(s * 16, 16), 16)
        tb[j, rows, :] = t
        return send([(tb.at[j, rows], tb.at[j, rows], m) for m in RING],
                    tb.at[j, pl.ds(0, 112)])

    def core_x(j):
        lc[j].wait()
        if j == 1:
            cb[1][own[1]] = jnp.concatenate([cst[1, 0:4, 0:256], cst[1, 0:4, 256:512]], 0)
        if j == 0:
            cb[0][own[0]] = jnp.concatenate(
                [cst[0, 0:2, 128 * k:128 * k + 128] for k in range(4)], 0)
        return send([(cb[j].at[own[j]], cb[j].at[own[j]], m) for m in XS],
                    cb[j].at[0, 0, pl.ds(0, 3), 0])

    def core_y(j, copies):
        landed(copies)
        view = cb[j].at[own[j][0], own[j][1], :, h]
        count = PIECES[j][1] - 1
        return send([(view, view, m) for m in YS[:count]], cb[j].at[0, pl.ds(0, count), :, 0])

    def core_z(j, copies):
        landed(copies)
        view = cb[j].at[own[j][0], :, :, h]
        count = PIECES[j][0] - 1
        return send([(view, view, m) for m in ZS4[:count]], cb[j].at[pl.ds(0, count), :, :, 0])

    def core_swap(j, copies):
        landed(copies)
        view = cb[j].at[:, :, :, h]
        return send([(view, view, 1)], view)

    def core_done(j, copies):
        landed(copies)
        value = cb[j][...]
        if j >= 2:
            cht[j, 0], cht[j, 1] = split(value.reshape(RANK, 2 * RANK).T)
            return
        width = PIECES[j][5]
        rows = 4 if j == 1 else 2
        value = value.reshape(RANK // 8, 8 // rows, 8, width)
        for k in range(512 // width):
            part = jnp.concatenate(
                [value[:, q, k * rows:(k + 1) * rows, :] for q in range(8 // rows)], 1)
            columns = pl.ds(k * width, width)
            cht[j, 0, columns], cht[j, 1, columns] = split(part.reshape(RANK, width).T)

    half_mine = pl.ds(pl.multiple_of(h * 128, 128), 128)
    half_other = pl.ds(pl.multiple_of((1 - h) * 128, 128), 128)

    def graph_swap(span):
        return send([(gloc.at[span, half_other], grh.at[span], 1)], grh.at[span])

    def chip_sum(span, copies):
        landed(copies)
        gs1[span] = gloc[span, half_mine, :] + grh[span]

    def piece(m, unit, size):
        at = x if unit == 2 else y
        return pl.ds(pl.multiple_of((at ^ (m // unit)) * size, size), size)

    def ring_scatter(span, copies, got):
        chip_sum(span, copies)
        return send([(gs1.at[span, piece(m, 2, 32)], got.at[i], m) for i, m in enumerate(XS)], got)

    def ring_gather(span, copies, got, full):
        landed(copies)
        full[:, h, x] = gs1[span, piece(0, 2, 32), :] + got[0] + got[1] + got[2]
        view = full.at[:, h, x]
        return send([(view, view, m) for m in XS], full.at[:, 0, pl.ds(0, 3)])

    def plane_scatter_y(span, copies, got):
        chip_sum(span, copies)
        return send([(gs1.at[span, piece(m, 8, 32)], got.at[i], m) for i, m in enumerate(YS)], got)

    def plane_scatter_x(span, copies, got, got_x):
        landed(copies)
        gs2[span] = gs1[span, piece(0, 8, 32), :] + got[0] + got[1] + got[2]
        return send([(gs2.at[span, piece(m, 2, 8)], got_x.at[i], m) for i, m in enumerate(XS)],
                    got_x)

    def plane_gather_x(span, copies, got_x, full):
        landed(copies)
        full[:, h, y, x] = gs2[span, piece(0, 2, 8), :] + got_x[0] + got_x[1] + got_x[2]
        view = full.at[:, h, y, x]
        return send([(view, view, m) for m in XS], full.at[:, 0, 0, pl.ds(0, 3)])

    def plane_gather_y(copies, full):
        landed(copies)
        view = full.at[:, h, y]
        return send([(view, view, m) for m in YS], full.at[:, 0, pl.ds(0, 3)])

    def full_swap(copies, full):
        landed(copies)
        view = full.at[:, h]
        return send([(view, view, 1)], view)

    def whole(full, g):
        return split(full[g].reshape(RANK, RANK))

    def plane_send(j, value):
        sb[j] = value
        return send([(sb.at[j], y1e.at[j, i], m) for i, m in enumerate(YS)], y1e.at[j])

    def plane_sum(j, value, copies):
        landed(copies)
        return value + y1e[j, 0] + y1e[j, 1] + y1e[j, 2]

    def exchange_up(j, value):
        sb[2 + j] = value
        return send([(sb.at[2 + j], eb.at[j, i], m) for i, m in enumerate(EXCHANGE[j])],
                    eb.at[j, pl.ds(0, len(EXCHANGE[j]))])

    S12, S0, S23, S13, S03 = (pl.ds(0, 1), pl.ds(1, 2), pl.ds(3, 1), pl.ds(4, 1), pl.ds(5, 1))

    lx.wait()
    set_state(xin[...].T)
    ready_p(4)
    yb[4] = mm(state(), p(4))
    pl.semaphore_wait(barrier, len(GREET))
    scatter4 = scatter(4)
    core4 = core_x(4)

    ready_p(1)
    ready_w(2)
    gloc[0] = mm(wt(2), p(1))
    plane12 = graph_swap(S12)
    ready_p(0)
    gloc[1] = mm(wt(2), p(0))
    ready_w(1)
    gloc[2] = mm(wt(1), p(0))
    sum4 = ring_sum(4, scatter4)
    exchange4 = exchange(4, sum4)
    core3 = core_x(3)
    core2 = core_x(2)
    core1 = core_x(1)
    core0 = core_x(0)
    plane0s = graph_swap(S0)
    plane12 = plane_scatter_y(S12, plane12, py12)
    ready_p(2)
    ready_w(3)
    gloc[3] = mm(wt(3), p(2))
    ring23 = graph_swap(S23)
    core4 = core_swap(4, core4)
    gloc[4] = mm(wt(3), p(1))
    ring13 = graph_swap(S13)
    core_done(4, core4)
    t4 = small(4, sum4, exchange4)
    gather4 = gather(4, t4)

    ready_p(3)
    ring23 = ring_scatter(S23, ring23, rx23)
    yb[3] = mm(state(), p(3))
    ring13 = ring_scatter(S13, ring13, rx13)
    ready_w(4)
    g34[...] = mm(wt(4), p(3))
    plane12 = plane_scatter_x(S12, plane12, py12, px12)
    core3 = core_y(3, core3)
    plane0s = plane_scatter_y(S0, plane0s, py0)
    core2 = core_y(2, core2)

    g34s = split(g34[...])
    landed(gather4)
    t4s = split(tb[4])
    yb[3] = yb[3] - mm(t4s, g34s)
    scatter3 = scatter(3)
    set_state(xt[...] - mm(t4s, wt(4)))
    yb[2] = mm(state(), p(2))
    scatter2 = scatter(2)
    ring23 = ring_gather(S23, ring23, rx23, gf23)
    yb[1] = mm(state(), p(1))
    scatter1 = scatter(1)
    plane12 = plane_gather_x(S12, plane12, px12, pf12)
    yb[0] = mm(state(), p(0))
    scatter0 = scatter(0)
    ring13 = ring_gather(S13, ring13, rx13, gf13)
    sum3 = ring_sum(3, scatter3)
    exchange3 = exchange(3, sum3)

    core3 = core_swap(3, core3)
    gloc[5] = mm(wt(3), p(0))
    ring03 = graph_swap(S03)
    ring23 = full_swap(ring23, gf23)
    core1 = core_y(1, core1)
    core_done(3, core3)
    plane12 = plane_gather_y(plane12, pf12)
    ring03 = ring_scatter(S03, ring03, rx03)
    sum2 = ring_sum(2, scatter2)
    landed(ring23)
    g23s = whole(gf23, 0)
    t3 = small(3, sum3, exchange3)
    t3s = split(t3)

    sum2 = sum2 - mm(t3s, g23s)
    exchange2 = exchange(2, sum2)
    gather3 = gather(3, t3)
    core2 = core_swap(2, core2)
    plane0s = plane_scatter_x(S0, plane0s, py0, px0)
    core0 = core_y(0, core0)
    core1 = core_z(1, core1)
    ring13 = full_swap(ring13, gf13)
    ring1 = ring_sum(1, scatter1)
    landed(ring13)
    ring1 = ring1 - mm(t3s, whole(gf13, 0))
    plane1 = plane_send(1, ring1)
    ring03 = ring_gather(S03, ring03, rx03, gf03)
    plane12 = full_swap(plane12, pf12)
    core_done(2, core2)
    plane0s = plane_gather_x(S0, plane0s, px0, pf0)
    core0 = core_z(0, core0)
    landed(plane12)
    g12s = whole(pf12, 0)
    t2 = small(2, sum2, exchange2)
    t2s = split(t2)
    plane1 = plane_sum(1, ring1, plane1)
    plane1 = plane1 - mm(t2s, g12s)
    exchange1 = exchange_up(1, plane1)

    gather2 = gather(2, t2)
    ring03 = full_swap(ring03, gf03)
    plane0s = plane_gather_y(plane0s, pf0)
    core1 = core_swap(1, core1)
    ring0 = ring_sum(0, scatter0)
    landed(ring03)
    ring0 = ring0 - mm(t3s, whole(gf03, 0))
    plane0 = plane_send(0, ring0)
    core_done(1, core1)
    core0 = core_swap(0, core0)
    landed(gather3)
    set_state(xt[...] - mm(split(tb[3]), wt(3)))
    plane0s = full_swap(plane0s, pf0)
    t1 = small(1, plane1, exchange1)
    plane0 = plane_sum(0, ring0, plane0)
    landed(plane0s)
    plane0 = plane0 - mm(t2s, whole(pf0, 0)) - mm(split(t1), whole(pf0, 1))
    exchange0 = exchange_up(0, plane0)

    gather1 = gather(1, t1)
    landed(gather2)
    set_state(xt[...] - mm(split(tb[2]), wt(2)))
    lw[0].wait()
    ws0[0], ws0[1] = split(win[0])
    core_done(0, core0)
    landed(gather1)
    x1[...] = (xt[...] - mm(split(tb[1]), wt(1))).T
    t0 = small(0, plane0, exchange0)
    gather0 = gather(0, t0)
    for copy in everything[:-1]:
        copy.wait_send()
    landed(gather0)
    t0s = split(tb[0])
    parts = []
    for k in range(4):
        rows = pl.ds(256 * k, 256)
        x1[rows, :] = x1[rows, :] - mm((ws0[0, rows], ws0[1, rows]), t0s, NT)
        parts.append(local(x1.at[rows], out.at[rows]))
    for copy in everything[-1:]:
        copy.wait_send()
    for copy in parts:
        copy.wait()
    assert used[0] == nsem, used[0]


NSEM = 57
NLOC = 20


def on_device(rhs, proj_bases, corr_bases, cores):
    any_space = pl.BlockSpec(memory_space=pl.ANY)
    v = pltpu.VMEM
    scratch = [
        v((ROWS, COLS), f32), v((5, ROWS, RANK), f32), v((5, ROWS, RANK), f32), v((2, 8, 512), f32),
        v((COLS, ROWS), f32), v((2, COLS, ROWS), bf16), v((ROWS, COLS), f32),
        v((5, 2, ROWS, RANK), bf16), v((4, 2, RANK, ROWS), bf16), v((2, ROWS, RANK), bf16),
        v((5, COLS, RANK), f32), v((5, 7, 16, RANK), f32), v((7, 16, RANK), f32),
        v((5, 7, 16, RANK), f32), v((5, COLS, RANK), f32),
        v(PIECES[4], f32), v(PIECES[3], f32), v(PIECES[2], f32), v(PIECES[1], f32), v(PIECES[0], f32),
        v((5, 2, 2 * RANK, RANK), bf16),
        v((RANK, RANK), f32), v((6, RANK, RANK), f32), v((6, 128, RANK), f32),
        v((6, 128, RANK), f32), v((3, 32, RANK), f32),
        v((3, 1, 32, RANK), f32), v((3, 1, 32, RANK), f32), v((3, 1, 32, RANK), f32),
        v((1, 2, 4, 32, RANK), f32), v((1, 2, 4, 32, RANK), f32), v((1, 2, 4, 32, RANK), f32),
        v((3, 1, 32, RANK), f32), v((3, 2, 32, RANK), f32),
        v((3, 1, 8, RANK), f32), v((3, 2, 8, RANK), f32),
        v((1, 2, 4, 4, 8, RANK), f32), v((2, 2, 4, 4, 8, RANK), f32),
        v((2, 3, 16, RANK), f32),
        pltpu.SemaphoreType.DMA((NLOC,)), pltpu.SemaphoreType.DMA((NSEM,)), pltpu.SemaphoreType.DMA((NSEM,)),
    ]
    return pl.pallas_call(
        functools.partial(kernel, NSEM),
        out_shape=jax.ShapeDtypeStruct((ROWS, COLS), f32),
        in_specs=[any_space] * 4,
        out_specs=any_space,
        scratch_shapes=scratch,
        compiler_params=pltpu.CompilerParams(
            collective_id=0, has_side_effects=True, vmem_limit_bytes=56 << 20),
        cost_estimate=pl.CostEstimate(flops=1 << 31, bytes_accessed=12 << 20, transcendentals=0),
    )(rhs, proj_bases, corr_bases, cores)


def solution(mesh):
    return jax.shard_map(
        on_device,
        mesh=mesh,
        in_specs=(
            P("leaf", None),
            P(None, "leaf", None),
            P(None, "leaf", None),
            P(None, "leaf", None),
        ),
        out_specs=P("leaf", None),
        check_vma=False,
    )
```

```python
import functools

import jax
import jax.numpy as jnp
from jax import lax
from jax.experimental import pallas as pl
from jax.experimental.pallas import tpu as pltpu
from jax.sharding import PartitionSpec as P

f32, bf16 = jnp.float32, jnp.bfloat16
ROWS, RANK, COLS = 1024, 256, 128
MESH = pl.DeviceIdType.MESH

RING = list(range(1, 8))
XS = [2, 4, 6]
YS = [8, 16, 24]
YZ = [8, 16, 24, 32, 40, 48, 56]
ZS4 = [32, 64, 96]
ZS8 = [32 * k for k in range(1, 8)]
EXCHANGE = {4: [8], 3: YS, 2: YZ, 1: ZS4, 0: ZS8}
GREET = sorted(set(RING + YS + YZ + ZS8))
PIECES = {4: (1, 1, 4, 2, 32, 512), 3: (1, 2, 4, 2, 16, 512), 2: (1, 4, 4, 2, 8, 512),
          1: (2, 4, 4, 2, 8, 256), 0: (4, 4, 4, 2, 8, 128)}

NN = ((1,), (0,))
NT = ((1,), (1,))


def split(a):
    high = a.astype(bf16)
    return high, (a - high.astype(f32)).astype(bf16)


def mm(a, b, dims=NN):
    def one(u, v):
        return lax.dot_general(u, v, (dims, ((), ())), preferred_element_type=f32)
    return one(a[0], b[0]) + (one(a[0], b[1]) + one(a[1], b[0]))


def kernel(nsem, rhs, proj, corr, cores, out, xin, pin, win, cst, xt, xts, x1, ps, wts, ws0,
           yb, rsb, sb, eb, tb, c4, c3, c2, c1, c0, cht, g34, gloc, grh, gs1, gs2,
           rx23, rx13, rx03, gf23, gf13, gf03, py12, py0, px12, px0, pf12, pf0, y1e,
           lsem, send_sem, recv_sem):
    me = lax.axis_index("leaf")
    h, x = me % 2, (me // 2) % 4
    y, z = (me // 8) % 4, me // 32
    s = me % 8
    cb = {4: c4, 3: c3, 2: c2, 1: c1, 0: c0}
    used = [0]
    everything = []

    def send(parts, total):
        k = used[0]
        used[0] += 1

        def describe(src, dst, mask):
            return pltpu.make_async_remote_copy(
                src_ref=src, dst_ref=dst, send_sem=send_sem.at[k], recv_sem=recv_sem.at[k],
                device_id=(me ^ mask,), device_id_type=MESH)

        for part in parts:
            describe(*part).start()
        group = describe(total, total, parts[0][2])
        everything.append(group)
        return group

    def landed(group):
        if group is not None:
            group.wait_recv()

    nlocal = [0]

    def local(src, dst):
        copy = pltpu.make_async_copy(src, dst, lsem.at[nlocal[0]])
        nlocal[0] += 1
        copy.start()
        return copy

    own = {j: (z % PIECES[j][0], y % PIECES[j][1], x, h) for j in PIECES}
    lp, lw, lc = {}, {}, {}

    def fetch_p(j):
        lp[j] = local(proj.at[j], pin.at[j])

    def fetch_w(k):
        lw[k] = local(corr.at[k], win.at[k])

    lx = local(rhs, xin)
    fetch_p(4)
    lc[4] = local(cores.at[4, pl.ds(0, 32)], c4.at[own[4]])
    fetch_p(1)
    fetch_w(2)
    fetch_p(0)
    fetch_w(1)
    fetch_p(2)
    fetch_w(3)
    lc[3] = local(cores.at[3, pl.ds(0, 16)], c3.at[own[3]])
    lc[2] = local(cores.at[2, pl.ds(0, 8)], c2.at[own[2]])
    lc[1] = local(cores.at[1, pl.ds(0, 8)], cst.at[1])
    lc[0] = local(cores.at[0, pl.ds(0, 8)], cst.at[0])
    fetch_p(3)
    fetch_w(4)
    fetch_w(0)

    barrier = pltpu.get_barrier_semaphore()
    for mask in GREET:
        pl.semaphore_signal(barrier, inc=1, device_id=(me ^ mask,), device_id_type=MESH)

    def ready_p(j):
        lp[j].wait()
        ps[j, 0], ps[j, 1] = split(pin[j])

    def ready_w(k):
        lw[k].wait()
        wts[k - 1, 0], wts[k - 1, 1] = split(win[k].T)

    def p(j):
        return ps[j, 0], ps[j, 1]

    def wt(k):
        return wts[k - 1, 0], wts[k - 1, 1]

    def state():
        return xts[0], xts[1]

    def set_state(value):
        xt[...] = value
        xts[0], xts[1] = split(value)

    def scatter(j):
        return send([(yb.at[j, pl.ds(pl.multiple_of((s ^ m) * 16, 16), 16)], rsb.at[j, m - 1], m)
                     for m in RING], rsb.at[j])

    def ring_sum(j, copies):
        landed(copies)
        total = yb[j, pl.ds(pl.multiple_of(s * 16, 16), 16), :]
        for m in RING:
            total = total + rsb[j, m - 1]
        return total

    def exchange(j, value):
        sb[2 + j] = value
        return send([(sb.at[2 + j], eb.at[j, i], m) for i, m in enumerate(EXCHANGE[j])],
                    eb.at[j, pl.ds(0, len(EXCHANGE[j]))])

    def small(j, value, copies):
        landed(copies)
        count = len(EXCHANGE[j])
        mine = value
        for i in range(count // 2):
            mine = mine + eb[j, i]
        other = eb[j, count // 2]
        for i in range(count // 2 + 1, count):
            other = other + eb[j, i]
        bit = 7 - j
        left = (me >> bit) % 2 == 0
        scale = (ROWS << bit) ** -0.5
        zl = jnp.where(left, mine, other) * scale
        zr = jnp.where(left, other, mine) * scale
        return mm(split(jnp.concatenate([zl, zr], 1)), (cht[j, 0], cht[j, 1]))

    def gather(j, t):
        rows = pl.ds(pl.multiple_of(s * 16, 16), 16)
        tb[j, rows, :] = t
        return send([(tb.at[j, rows], tb.at[j, rows], m) for m in RING],
                    tb.at[j, pl.ds(0, 112)])

    def core_z(j):
        lc[j].wait()
        if j == 1:
            cb[1][own[1]] = jnp.concatenate([cst[1, 0:4, 0:256], cst[1, 0:4, 256:512]], 0)
        else:
            cb[0][own[0]] = jnp.concatenate(
                [cst[0, 0:2, 128 * k:128 * k + 128] for k in range(4)], 0)
        view, count = cb[j].at[own[j]], PIECES[j][0] - 1
        return send([(view, view, m) for m in ZS4[:count]], cb[j].at[pl.ds(0, count), 0, 0, 0])

    def core_x(j, copies=None):
        if copies is None:
            lc[j].wait()
        landed(copies)
        view = cb[j].at[:, own[j][1], x, h]
        return send([(view, view, m) for m in XS], cb[j].at[:, 0, pl.ds(0, 3), 0])

    def core_y(j, copies):
        landed(copies)
        view, count = cb[j].at[:, own[j][1], :, h], PIECES[j][1] - 1
        return send([(view, view, m) for m in YS[:count]], cb[j].at[:, pl.ds(0, count), :, 0])

    def core_swap(j, copies):
        landed(copies)
        view = cb[j].at[:, :, :, h]
        return send([(view, view, 1)], view)

    def core_done(j, copies):
        landed(copies)
        value = cb[j][...]
        if j >= 2:
            cht[j, 0], cht[j, 1] = split(value.reshape(RANK, 2 * RANK).T)
            return
        width = PIECES[j][5]
        rows = 4 if j == 1 else 2
        value = value.reshape(RANK // 8, 8 // rows, 8, width)
        for k in range(512 // width):
            part = jnp.concatenate(
                [value[:, q, k * rows:(k + 1) * rows, :] for q in range(8 // rows)], 1)
            columns = pl.ds(k * width, width)
            cht[j, 0, columns], cht[j, 1, columns] = split(part.reshape(RANK, width).T)

    half_mine = pl.ds(pl.multiple_of(h * 128, 128), 128)
    half_other = pl.ds(pl.multiple_of((1 - h) * 128, 128), 128)

    def graph_swap(span):
        return send([(gloc.at[span, half_other], grh.at[span], 1)], grh.at[span])

    def chip_sum(span, copies):
        landed(copies)
        gs1[span] = gloc[span, half_mine, :] + grh[span]

    def piece(m, unit, size):
        at = x if unit == 2 else y
        return pl.ds(pl.multiple_of((at ^ (m // unit)) * size, size), size)

    def ring_scatter(span, copies, got):
        chip_sum(span, copies)
        return send([(gs1.at[span, piece(m, 2, 32)], got.at[i], m) for i, m in enumerate(XS)], got)

    def ring_gather(span, copies, got, full):
        landed(copies)
        full[:, h, x] = gs1[span, piece(0, 2, 32), :] + got[0] + got[1] + got[2]
        view = full.at[:, h, x]
        return send([(view, view, m) for m in XS], full.at[:, 0, pl.ds(0, 3)])

    def plane_scatter_y(span, copies, got):
        chip_sum(span, copies)
        return send([(gs1.at[span, piece(m, 8, 32)], got.at[i], m) for i, m in enumerate(YS)], got)

    def plane_scatter_x(span, copies, got, got_x):
        landed(copies)
        gs2[span] = gs1[span, piece(0, 8, 32), :] + got[0] + got[1] + got[2]
        return send([(gs2.at[span, piece(m, 2, 8)], got_x.at[i], m) for i, m in enumerate(XS)],
                    got_x)

    def plane_gather_x(span, copies, got_x, full):
        landed(copies)
        full[:, h, y, x] = gs2[span, piece(0, 2, 8), :] + got_x[0] + got_x[1] + got_x[2]
        view = full.at[:, h, y, x]
        return send([(view, view, m) for m in XS], full.at[:, 0, 0, pl.ds(0, 3)])

    def plane_gather_y(copies, full):
        landed(copies)
        view = full.at[:, h, y]
        return send([(view, view, m) for m in YS], full.at[:, 0, pl.ds(0, 3)])

    def full_swap(copies, full):
        landed(copies)
        view = full.at[:, h]
        return send([(view, view, 1)], view)

    def whole(full, g):
        return split(full[g].reshape(RANK, RANK))

    def plane_send(j, value):
        sb[j] = value
        return send([(sb.at[j], y1e.at[j, i], m) for i, m in enumerate(YS)], y1e.at[j])

    def plane_sum(j, value, copies):
        landed(copies)
        return value + y1e[j, 0] + y1e[j, 1] + y1e[j, 2]

    def exchange_up(j, value):
        sb[2 + j] = value
        return send([(sb.at[2 + j], eb.at[j, i], m) for i, m in enumerate(EXCHANGE[j])],
                    eb.at[j, pl.ds(0, len(EXCHANGE[j]))])

    S12, S0, S23, S13, S03 = (pl.ds(0, 1), pl.ds(1, 2), pl.ds(3, 1), pl.ds(4, 1), pl.ds(5, 1))

    lx.wait()
    set_state(xin[...].T)
    ready_p(4)
    yb[4] = mm(state(), p(4))
    pl.semaphore_wait(barrier, len(GREET))
    scatter4 = scatter(4)
    core4 = core_x(4)
    core1 = core_z(1)
    core0 = core_z(0)

    ready_p(1)
    ready_w(2)
    gloc[0] = mm(wt(2), p(1))
    plane12 = graph_swap(S12)
    ready_p(0)
    gloc[1] = mm(wt(2), p(0))
    ready_w(1)
    gloc[2] = mm(wt(1), p(0))
    sum4 = ring_sum(4, scatter4)
    exchange4 = exchange(4, sum4)
    core3 = core_x(3)
    core2 = core_x(2)
    core1 = core_x(1, core1)
    core0 = core_x(0, core0)
    plane0s = graph_swap(S0)
    plane12 = plane_scatter_y(S12, plane12, py12)
    ready_p(2)
    ready_w(3)
    gloc[3] = mm(wt(3), p(2))
    ring23 = graph_swap(S23)
    core4 = core_swap(4, core4)
    gloc[4] = mm(wt(3), p(1))
    ring13 = graph_swap(S13)
    core_done(4, core4)
    t4 = small(4, sum4, exchange4)
    gather4 = gather(4, t4)

    ready_p(3)
    ring23 = ring_scatter(S23, ring23, rx23)
    yb[3] = mm(state(), p(3))
    ring13 = ring_scatter(S13, ring13, rx13)
    ready_w(4)
    g34[...] = mm(wt(4), p(3))
    plane12 = plane_scatter_x(S12, plane12, py12, px12)
    core2 = core_y(2, core2)
    core3 = core_y(3, core3)
    plane0s = plane_scatter_y(S0, plane0s, py0)

    gloc[5] = mm(wt(3), p(0))
    ring03 = graph_swap(S03)
    g34s = split(g34[...])
    landed(gather4)
    t4s = split(tb[4])
    yb[3] = yb[3] - mm(t4s, g34s)
    scatter3 = scatter(3)
    set_state(xt[...] - mm(t4s, wt(4)))
    yb[2] = mm(state(), p(2))
    scatter2 = scatter(2)
    ring23 = ring_gather(S23, ring23, rx23, gf23)
    yb[1] = mm(state(), p(1))
    scatter1 = scatter(1)
    plane12 = plane_gather_x(S12, plane12, px12, pf12)
    yb[0] = mm(state(), p(0))
    scatter0 = scatter(0)
    ring13 = ring_gather(S13, ring13, rx13, gf13)
    sum3 = ring_sum(3, scatter3)
    exchange3 = exchange(3, sum3)

    core3 = core_swap(3, core3)
    ring23 = full_swap(ring23, gf23)
    core1 = core_y(1, core1)
    core_done(3, core3)
    core2 = core_swap(2, core2)
    plane12 = plane_gather_y(plane12, pf12)
    ring03 = ring_scatter(S03, ring03, rx03)
    plane0s = plane_scatter_x(S0, plane0s, py0, px0)
    sum2 = ring_sum(2, scatter2)
    landed(ring23)
    g23s = whole(gf23, 0)
    t3 = small(3, sum3, exchange3)
    t3s = split(t3)

    sum2 = sum2 - mm(t3s, g23s)
    exchange2 = exchange(2, sum2)
    gather3 = gather(3, t3)
    core0 = core_y(0, core0)
    ring13 = full_swap(ring13, gf13)
    plane0s = plane_gather_x(S0, plane0s, px0, pf0)
    ring1 = ring_sum(1, scatter1)
    landed(ring13)
    ring1 = ring1 - mm(t3s, whole(gf13, 0))
    plane1 = plane_send(1, ring1)
    ring03 = ring_gather(S03, ring03, rx03, gf03)
    plane12 = full_swap(plane12, pf12)
    core_done(2, core2)
    plane0s = plane_gather_y(plane0s, pf0)
    landed(plane12)
    g12s = whole(pf12, 0)
    t2 = small(2, sum2, exchange2)
    t2s = split(t2)
    plane1 = plane_sum(1, ring1, plane1)
    plane1 = plane1 - mm(t2s, g12s)
    exchange1 = exchange_up(1, plane1)

    gather2 = gather(2, t2)
    ring03 = full_swap(ring03, gf03)
    core1 = core_swap(1, core1)
    ring0 = ring_sum(0, scatter0)
    landed(ring03)
    ring0 = ring0 - mm(t3s, whole(gf03, 0))
    plane0 = plane_send(0, ring0)
    core_done(1, core1)
    core0 = core_swap(0, core0)
    landed(gather3)
    set_state(xt[...] - mm(split(tb[3]), wt(3)))
    plane0s = full_swap(plane0s, pf0)
    t1 = small(1, plane1, exchange1)
    plane0 = plane_sum(0, ring0, plane0)
    landed(plane0s)
    plane0 = plane0 - mm(t2s, whole(pf0, 0)) - mm(split(t1), whole(pf0, 1))
    exchange0 = exchange_up(0, plane0)

    gather1 = gather(1, t1)
    landed(gather2)
    set_state(xt[...] - mm(split(tb[2]), wt(2)))
    lw[0].wait()
    ws0[0], ws0[1] = split(win[0])
    core_done(0, core0)
    landed(gather1)
    x1[...] = (xt[...] - mm(split(tb[1]), wt(1))).T
    t0 = small(0, plane0, exchange0)
    gather0 = gather(0, t0)
    for copy in everything[:-1]:
        copy.wait_send()
    landed(gather0)
    t0s = split(tb[0])
    parts = []
    for k in range(4):
        rows = pl.ds(256 * k, 256)
        x1[rows, :] = x1[rows, :] - mm((ws0[0, rows], ws0[1, rows]), t0s, NT)
        parts.append(local(x1.at[rows], out.at[rows]))
    for copy in everything[-1:]:
        copy.wait_send()
    for copy in parts:
        copy.wait()
    assert used[0] == nsem, used[0]


NSEM = 57
NLOC = 20


def on_device(rhs, proj_bases, corr_bases, cores):
    any_space = pl.BlockSpec(memory_space=pl.ANY)
    v = pltpu.VMEM
    scratch = [
        v((ROWS, COLS), f32), v((5, ROWS, RANK), f32), v((5, ROWS, RANK), f32), v((2, 8, 512), f32),
        v((COLS, ROWS), f32), v((2, COLS, ROWS), bf16), v((ROWS, COLS), f32),
        v((5, 2, ROWS, RANK), bf16), v((4, 2, RANK, ROWS), bf16), v((2, ROWS, RANK), bf16),
        v((5, COLS, RANK), f32), v((5, 7, 16, RANK), f32), v((7, 16, RANK), f32),
        v((5, 7, 16, RANK), f32), v((5, COLS, RANK), f32),
        v(PIECES[4], f32), v(PIECES[3], f32), v(PIECES[2], f32), v(PIECES[1], f32), v(PIECES[0], f32),
        v((5, 2, 2 * RANK, RANK), bf16),
        v((RANK, RANK), f32), v((6, RANK, RANK), f32), v((6, 128, RANK), f32),
        v((6, 128, RANK), f32), v((3, 32, RANK), f32),
        v((3, 1, 32, RANK), f32), v((3, 1, 32, RANK), f32), v((3, 1, 32, RANK), f32),
        v((1, 2, 4, 32, RANK), f32), v((1, 2, 4, 32, RANK), f32), v((1, 2, 4, 32, RANK), f32),
        v((3, 1, 32, RANK), f32), v((3, 2, 32, RANK), f32),
        v((3, 1, 8, RANK), f32), v((3, 2, 8, RANK), f32),
        v((1, 2, 4, 4, 8, RANK), f32), v((2, 2, 4, 4, 8, RANK), f32),
        v((2, 3, 16, RANK), f32),
        pltpu.SemaphoreType.DMA((NLOC,)), pltpu.SemaphoreType.DMA((NSEM,)), pltpu.SemaphoreType.DMA((NSEM,)),
    ]
    return pl.pallas_call(
        functools.partial(kernel, NSEM),
        out_shape=jax.ShapeDtypeStruct((ROWS, COLS), f32),
        in_specs=[any_space] * 4,
        out_specs=any_space,
        scratch_shapes=scratch,
        compiler_params=pltpu.CompilerParams(
            collective_id=0, has_side_effects=True, vmem_limit_bytes=56 << 20),
        cost_estimate=pl.CostEstimate(flops=1 << 31, bytes_accessed=12 << 20, transcendentals=0),
    )(rhs, proj_bases, corr_bases, cores)


def solution(mesh):
    return jax.shard_map(
        on_device,
        mesh=mesh,
        in_specs=(
            P("leaf", None),
            P(None, "leaf", None),
            P(None, "leaf", None),
            P(None, "leaf", None),
        ),
        out_specs=P("leaf", None),
        check_vma=False,
    )
```

```python
import functools

import jax
import jax.numpy as jnp
from jax import lax
from jax.experimental import pallas as pl
from jax.experimental.pallas import tpu as pltpu
from jax.sharding import PartitionSpec as P

f32, bf16 = jnp.float32, jnp.bfloat16
ROWS, RANK, COLS = 1024, 256, 128
MESH = pl.DeviceIdType.MESH

RING = list(range(1, 8))
XS = [2, 4, 6]
YS = [8, 16, 24]
YZ = [8, 16, 24, 32, 40, 48, 56]
ZS4 = [32, 64, 96]
ZS8 = [32 * k for k in range(1, 8)]
EXCHANGE = {4: [8], 3: YS, 2: YZ, 1: ZS4, 0: ZS8}
GREET = sorted(set(RING + YS + YZ + ZS8))
PIECES = {4: (1, 1, 4, 2, 32, 512), 3: (1, 2, 4, 2, 16, 512), 2: (1, 4, 4, 2, 8, 512),
          1: (2, 4, 4, 2, 8, 256), 0: (4, 4, 4, 2, 8, 128)}

NN = ((1,), (0,))
NT = ((1,), (1,))


def split(a):
    high = a.astype(bf16)
    return high, (a - high.astype(f32)).astype(bf16)


def mm(a, b, dims=NN):
    def one(u, v):
        return lax.dot_general(u, v, (dims, ((), ())), preferred_element_type=f32)
    return one(a[0], b[0]) + (one(a[0], b[1]) + one(a[1], b[0]))


def kernel(nsem, rhs, proj, corr, cores, out, xin, pin, win, cst, xt, xts, x1, ps, wts, ws0,
           yb, rsb, sb, eb, tb, c4, c3, c2, c1, c0, cht, g34, gloc, grh, gs1, gs2,
           rx23, rx13, rx03, gf23, gf13, gf03, py12, py0, px12, px0, pf12, pf0, y1e,
           lsem, send_sem, recv_sem):
    me = lax.axis_index("leaf")
    h, x = me % 2, (me // 2) % 4
    y, z = (me // 8) % 4, me // 32
    s = me % 8
    cb = {4: c4, 3: c3, 2: c2, 1: c1, 0: c0}
    used = [0]
    everything = []

    def send(parts, total):
        k = used[0]
        used[0] += 1

        def describe(src, dst, mask):
            return pltpu.make_async_remote_copy(
                src_ref=src, dst_ref=dst, send_sem=send_sem.at[k], recv_sem=recv_sem.at[k],
                device_id=(me ^ mask,), device_id_type=MESH)

        for part in parts:
            describe(*part).start()
        group = describe(total, total, parts[0][2])
        everything.append(group)
        return group

    def landed(group):
        if group is not None:
            group.wait_recv()

    nlocal = [0]

    def local(src, dst):
        copy = pltpu.make_async_copy(src, dst, lsem.at[nlocal[0]])
        nlocal[0] += 1
        copy.start()
        return copy

    own = {j: (z % PIECES[j][0], y % PIECES[j][1], x, h) for j in PIECES}
    lp, lw, lc = {}, {}, {}

    def fetch_p(j):
        lp[j] = local(proj.at[j], pin.at[j])

    def fetch_w(k):
        lw[k] = local(corr.at[k], win.at[k])

    lx = local(rhs, xin)
    fetch_p(4)
    lc[4] = local(cores.at[4, pl.ds(0, 32)], c4.at[own[4]])
    fetch_p(1)
    fetch_w(2)
    fetch_p(0)
    fetch_w(1)
    fetch_p(2)
    fetch_w(3)
    lc[3] = local(cores.at[3, pl.ds(0, 16)], c3.at[own[3]])
    lc[2] = local(cores.at[2, pl.ds(0, 8)], c2.at[own[2]])
    lc[1] = local(cores.at[1, pl.ds(0, 8)], cst.at[1])
    lc[0] = local(cores.at[0, pl.ds(0, 8)], cst.at[0])
    fetch_p(3)
    fetch_w(4)
    fetch_w(0)

    barrier = pltpu.get_barrier_semaphore()
    for mask in GREET:
        pl.semaphore_signal(barrier, inc=1, device_id=(me ^ mask,), device_id_type=MESH)

    def ready_p(j):
        lp[j].wait()
        ps[j, 0], ps[j, 1] = split(pin[j])

    def ready_w(k):
        lw[k].wait()
        wts[k - 1, 0], wts[k - 1, 1] = split(win[k].T)

    def p(j):
        return ps[j, 0], ps[j, 1]

    def wt(k):
        return wts[k - 1, 0], wts[k - 1, 1]

    def state():
        return xts[0], xts[1]

    def set_state(value):
        xt[...] = value
        xts[0], xts[1] = split(value)

    def scatter(j):
        return send([(yb.at[j, pl.ds(pl.multiple_of((s ^ m) * 16, 16), 16)], rsb.at[j, m - 1], m)
                     for m in RING], rsb.at[j])

    def ring_sum(j, copies):
        landed(copies)
        total = yb[j, pl.ds(pl.multiple_of(s * 16, 16), 16), :]
        for m in RING:
            total = total + rsb[j, m - 1]
        return total

    def exchange(j, value):
        sb[2 + j] = value
        return send([(sb.at[2 + j], eb.at[j, i], m) for i, m in enumerate(EXCHANGE[j])],
                    eb.at[j, pl.ds(0, len(EXCHANGE[j]))])

    def small(j, value, copies):
        landed(copies)
        count = len(EXCHANGE[j])
        mine = value
        for i in range(count // 2):
            mine = mine + eb[j, i]
        other = eb[j, count // 2]
        for i in range(count // 2 + 1, count):
            other = other + eb[j, i]
        bit = 7 - j
        left = (me >> bit) % 2 == 0
        scale = (ROWS << bit) ** -0.5
        zl = jnp.where(left, mine, other) * scale
        zr = jnp.where(left, other, mine) * scale
        return mm(split(jnp.concatenate([zl, zr], 1)), (cht[j, 0], cht[j, 1]))

    def gather(j, t):
        rows = pl.ds(pl.multiple_of(s * 16, 16), 16)
        tb[j, rows, :] = t
        return send([(tb.at[j, rows], tb.at[j, rows], m) for m in RING],
                    tb.at[j, pl.ds(0, 112)])

    def core_z(j):
        lc[j].wait()
        if j == 1:
            cb[1][own[1]] = jnp.concatenate([cst[1, 0:4, 0:256], cst[1, 0:4, 256:512]], 0)
        else:
            cb[0][own[0]] = jnp.concatenate(
                [cst[0, 0:2, 128 * k:128 * k + 128] for k in range(4)], 0)
        view, count = cb[j].at[own[j]], PIECES[j][0] - 1
        return send([(view, view, m) for m in ZS4[:count]], cb[j].at[pl.ds(0, count), 0, 0, 0])

    def core_x(j, copies=None):
        if copies is None:
            lc[j].wait()
        landed(copies)
        view = cb[j].at[:, own[j][1], x, h]
        return send([(view, view, m) for m in XS], cb[j].at[:, 0, pl.ds(0, 3), 0])

    def core_y(j, copies):
        landed(copies)
        view, count = cb[j].at[:, own[j][1], :, h], PIECES[j][1] - 1
        return send([(view, view, m) for m in YS[:count]], cb[j].at[:, pl.ds(0, count), :, 0])

    def core_swap(j, copies):
        landed(copies)
        view = cb[j].at[:, :, :, h]
        return send([(view, view, 1)], view)

    def core_done(j, copies):
        landed(copies)
        value = cb[j][...]
        if j >= 2:
            cht[j, 0], cht[j, 1] = split(value.reshape(RANK, 2 * RANK).T)
            return
        width = PIECES[j][5]
        rows = 4 if j == 1 else 2
        value = value.reshape(RANK // 8, 8 // rows, 8, width)
        for k in range(512 // width):
            part = jnp.concatenate(
                [value[:, q, k * rows:(k + 1) * rows, :] for q in range(8 // rows)], 1)
            columns = pl.ds(k * width, width)
            cht[j, 0, columns], cht[j, 1, columns] = split(part.reshape(RANK, width).T)

    half_mine = pl.ds(pl.multiple_of(h * 128, 128), 128)
    half_other = pl.ds(pl.multiple_of((1 - h) * 128, 128), 128)

    def graph_swap(span):
        return send([(gloc.at[span, half_other], grh.at[span], 1)], grh.at[span])

    def chip_sum(span, copies):
        landed(copies)
        gs1[span] = gloc[span, half_mine, :] + grh[span]

    def piece(m, unit, size):
        at = x if unit == 2 else y
        return pl.ds(pl.multiple_of((at ^ (m // unit)) * size, size), size)

    def ring_scatter(span, copies, got):
        chip_sum(span, copies)
        return send([(gs1.at[span, piece(m, 2, 32)], got.at[i], m) for i, m in enumerate(XS)], got)

    def ring_gather(span, copies, got, full):
        landed(copies)
        full[:, h, x] = gs1[span, piece(0, 2, 32), :] + got[0] + got[1] + got[2]
        view = full.at[:, h, x]
        return send([(view, view, m) for m in XS], full.at[:, 0, pl.ds(0, 3)])

    def plane_scatter_y(span, copies, got):
        chip_sum(span, copies)
        return send([(gs1.at[span, piece(m, 8, 32)], got.at[i], m) for i, m in enumerate(YS)], got)

    def plane_scatter_x(span, copies, got, got_x):
        landed(copies)
        gs2[span] = gs1[span, piece(0, 8, 32), :] + got[0] + got[1] + got[2]
        return send([(gs2.at[span, piece(m, 2, 8)], got_x.at[i], m) for i, m in enumerate(XS)],
                    got_x)

    def plane_gather_x(span, copies, got_x, full):
        landed(copies)
        full[:, h, y, x] = gs2[span, piece(0, 2, 8), :] + got_x[0] + got_x[1] + got_x[2]
        view = full.at[:, h, y, x]
        return send([(view, view, m) for m in XS], full.at[:, 0, 0, pl.ds(0, 3)])

    def plane_gather_y(copies, full):
        landed(copies)
        view = full.at[:, h, y]
        return send([(view, view, m) for m in YS], full.at[:, 0, pl.ds(0, 3)])

    def full_swap(copies, full):
        landed(copies)
        view = full.at[:, h]
        return send([(view, view, 1)], view)

    def whole(full, g):
        return split(full[g].reshape(RANK, RANK))

    def plane_send(j, value):
        sb[j] = value
        return send([(sb.at[j], y1e.at[j, i], m) for i, m in enumerate(YS)], y1e.at[j])

    def plane_sum(j, value, copies):
        landed(copies)
        return value + y1e[j, 0] + y1e[j, 1] + y1e[j, 2]

    def exchange_up(j, value):
        sb[2 + j] = value
        return send([(sb.at[2 + j], eb.at[j, i], m) for i, m in enumerate(EXCHANGE[j])],
                    eb.at[j, pl.ds(0, len(EXCHANGE[j]))])

    S12, S0, S23, S13, S03 = (pl.ds(0, 1), pl.ds(1, 2), pl.ds(3, 1), pl.ds(4, 1), pl.ds(5, 1))

    lx.wait()
    set_state(xin[...].T)
    ready_p(4)
    yb[4] = mm(state(), p(4))
    pl.semaphore_wait(barrier, len(GREET))
    scatter4 = scatter(4)
    core4 = core_x(4)
    core1 = core_z(1)
    core0 = core_z(0)

    ready_p(1)
    ready_w(2)
    gloc[0] = mm(wt(2), p(1))
    plane12 = graph_swap(S12)
    ready_p(0)
    gloc[1] = mm(wt(2), p(0))
    ready_w(1)
    gloc[2] = mm(wt(1), p(0))
    sum4 = ring_sum(4, scatter4)
    exchange4 = exchange(4, sum4)
    core3 = core_x(3)
    core2 = core_x(2)
    core1 = core_x(1, core1)
    core0 = core_x(0, core0)
    plane0s = graph_swap(S0)
    plane12 = plane_scatter_y(S12, plane12, py12)
    ready_p(2)
    ready_w(3)
    gloc[3] = mm(wt(3), p(2))
    ring23 = graph_swap(S23)
    core4 = core_swap(4, core4)
    gloc[4] = mm(wt(3), p(1))
    ring13 = graph_swap(S13)
    core_done(4, core4)
    t4 = small(4, sum4, exchange4)
    gather4 = gather(4, t4)
    plane0s = plane_scatter_y(S0, plane0s, py0)

    ready_p(3)
    ring23 = ring_scatter(S23, ring23, rx23)
    yb[3] = mm(state(), p(3))
    ring13 = ring_scatter(S13, ring13, rx13)
    ready_w(4)
    g34[...] = mm(wt(4), p(3))
    plane12 = plane_scatter_x(S12, plane12, py12, px12)
    core2 = core_y(2, core2)
    core3 = core_y(3, core3)

    gloc[5] = mm(wt(3), p(0))
    ring03 = graph_swap(S03)
    g34s = split(g34[...])
    landed(gather4)
    t4s = split(tb[4])
    yb[3] = yb[3] - mm(t4s, g34s)
    scatter3 = scatter(3)
    set_state(xt[...] - mm(t4s, wt(4)))
    yb[2] = mm(state(), p(2))
    scatter2 = scatter(2)
    ring23 = ring_gather(S23, ring23, rx23, gf23)
    yb[1] = mm(state(), p(1))
    scatter1 = scatter(1)
    plane12 = plane_gather_x(S12, plane12, px12, pf12)
    yb[0] = mm(state(), p(0))
    scatter0 = scatter(0)
    ring13 = ring_gather(S13, ring13, rx13, gf13)
    sum3 = ring_sum(3, scatter3)
    exchange3 = exchange(3, sum3)

    core3 = core_swap(3, core3)
    ring23 = full_swap(ring23, gf23)
    core1 = core_y(1, core1)
    core_done(3, core3)
    core2 = core_swap(2, core2)
    plane12 = plane_gather_y(plane12, pf12)
    ring03 = ring_scatter(S03, ring03, rx03)
    plane0s = plane_scatter_x(S0, plane0s, py0, px0)
    sum2 = ring_sum(2, scatter2)
    landed(ring23)
    g23s = whole(gf23, 0)
    t3 = small(3, sum3, exchange3)
    t3s = split(t3)

    sum2 = sum2 - mm(t3s, g23s)
    exchange2 = exchange(2, sum2)
    gather3 = gather(3, t3)
    core0 = core_y(0, core0)
    ring13 = full_swap(ring13, gf13)
    plane0s = plane_gather_x(S0, plane0s, px0, pf0)
    ring1 = ring_sum(1, scatter1)
    landed(ring13)
    ring1 = ring1 - mm(t3s, whole(gf13, 0))
    plane1 = plane_send(1, ring1)
    ring03 = ring_gather(S03, ring03, rx03, gf03)
    plane12 = full_swap(plane12, pf12)
    core_done(2, core2)
    plane0s = plane_gather_y(plane0s, pf0)
    landed(plane12)
    g12s = whole(pf12, 0)
    t2 = small(2, sum2, exchange2)
    t2s = split(t2)
    plane1 = plane_sum(1, ring1, plane1)
    plane1 = plane1 - mm(t2s, g12s)
    exchange1 = exchange_up(1, plane1)

    gather2 = gather(2, t2)
    ring03 = full_swap(ring03, gf03)
    core1 = core_swap(1, core1)
    ring0 = ring_sum(0, scatter0)
    landed(ring03)
    ring0 = ring0 - mm(t3s, whole(gf03, 0))
    plane0 = plane_send(0, ring0)
    core_done(1, core1)
    core0 = core_swap(0, core0)
    landed(gather3)
    set_state(xt[...] - mm(split(tb[3]), wt(3)))
    plane0s = full_swap(plane0s, pf0)
    t1 = small(1, plane1, exchange1)
    plane0 = plane_sum(0, ring0, plane0)
    landed(plane0s)
    plane0 = plane0 - mm(t2s, whole(pf0, 0)) - mm(split(t1), whole(pf0, 1))
    exchange0 = exchange_up(0, plane0)

    gather1 = gather(1, t1)
    landed(gather2)
    set_state(xt[...] - mm(split(tb[2]), wt(2)))
    lw[0].wait()
    ws0[0], ws0[1] = split(win[0])
    core_done(0, core0)
    landed(gather1)
    x1[...] = (xt[...] - mm(split(tb[1]), wt(1))).T
    t0 = small(0, plane0, exchange0)
    gather0 = gather(0, t0)
    for copy in everything[:-1]:
        copy.wait_send()
    landed(gather0)
    t0s = split(tb[0])
    parts = []
    for k in range(4):
        rows = pl.ds(256 * k, 256)
        x1[rows, :] = x1[rows, :] - mm((ws0[0, rows], ws0[1, rows]), t0s, NT)
        parts.append(local(x1.at[rows], out.at[rows]))
    for copy in everything[-1:]:
        copy.wait_send()
    for copy in parts:
        copy.wait()
    assert used[0] == nsem, used[0]


NSEM = 57
NLOC = 20


def on_device(rhs, proj_bases, corr_bases, cores):
    any_space = pl.BlockSpec(memory_space=pl.ANY)
    v = pltpu.VMEM
    scratch = [
        v((ROWS, COLS), f32), v((5, ROWS, RANK), f32), v((5, ROWS, RANK), f32), v((2, 8, 512), f32),
        v((COLS, ROWS), f32), v((2, COLS, ROWS), bf16), v((ROWS, COLS), f32),
        v((5, 2, ROWS, RANK), bf16), v((4, 2, RANK, ROWS), bf16), v((2, ROWS, RANK), bf16),
        v((5, COLS, RANK), f32), v((5, 7, 16, RANK), f32), v((7, 16, RANK), f32),
        v((5, 7, 16, RANK), f32), v((5, COLS, RANK), f32),
        v(PIECES[4], f32), v(PIECES[3], f32), v(PIECES[2], f32), v(PIECES[1], f32), v(PIECES[0], f32),
        v((5, 2, 2 * RANK, RANK), bf16),
        v((RANK, RANK), f32), v((6, RANK, RANK), f32), v((6, 128, RANK), f32),
        v((6, 128, RANK), f32), v((3, 32, RANK), f32),
        v((3, 1, 32, RANK), f32), v((3, 1, 32, RANK), f32), v((3, 1, 32, RANK), f32),
        v((1, 2, 4, 32, RANK), f32), v((1, 2, 4, 32, RANK), f32), v((1, 2, 4, 32, RANK), f32),
        v((3, 1, 32, RANK), f32), v((3, 2, 32, RANK), f32),
        v((3, 1, 8, RANK), f32), v((3, 2, 8, RANK), f32),
        v((1, 2, 4, 4, 8, RANK), f32), v((2, 2, 4, 4, 8, RANK), f32),
        v((2, 3, 16, RANK), f32),
        pltpu.SemaphoreType.DMA((NLOC,)), pltpu.SemaphoreType.DMA((NSEM,)), pltpu.SemaphoreType.DMA((NSEM,)),
    ]
    return pl.pallas_call(
        functools.partial(kernel, NSEM),
        out_shape=jax.ShapeDtypeStruct((ROWS, COLS), f32),
        in_specs=[any_space] * 4,
        out_specs=any_space,
        scratch_shapes=scratch,
        compiler_params=pltpu.CompilerParams(
            collective_id=0, has_side_effects=True, vmem_limit_bytes=56 << 20),
        cost_estimate=pl.CostEstimate(flops=1 << 31, bytes_accessed=12 << 20, transcendentals=0),
    )(rhs, proj_bases, corr_bases, cores)


def solution(mesh):
    return jax.shard_map(
        on_device,
        mesh=mesh,
        in_specs=(
            P("leaf", None),
            P(None, "leaf", None),
            P(None, "leaf", None),
            P(None, "leaf", None),
        ),
        out_specs=P("leaf", None),
        check_vma=False,
    )
```
